32 devices in a mesh: tm: 4 (over y, core), height: 2 (over x), head: 4 (over z).
Axes of the slice: x: 2, y: 2, z: 4, core: 2. Of those that a mesh axis runs over, the one named last changes fastest.
Arguments:
- queries: bfloat16 [3072, 3072], P(('tm', 'height'), 'head'), may hold values from -6 to 6
- keys: bfloat16 [3072, 3072], P(('tm', 'height'), 'head'), may hold values from -12 to 12
- values: bfloat16 [3072, 3072], P(('tm', 'height'), 'head'), may hold values from -6 to 6
- out_grad: bfloat16 [3072, 3072], P(('tm', 'height'), 'head'), may hold values from -6 to 6
- out_weight: bfloat16 [3072, 3072], P(None, 'head'), may hold values from -0.109375 to 0.109375
- window: int32 [8, 27], P(('tm', 'height')), may hold values from 0 to 1, as said below
- counts: int32 [8], P(('tm', 'height')), may hold values from 96 to 384, as said below
Outputs:
- query_grad: bfloat16 [3072, 3072], P(('tm', 'height'), 'head')
- key_grad: bfloat16 [3072, 3072], P(('tm', 'height'), 'head')
- value_grad: bfloat16 [3072, 3072], P(('tm', 'height'), 'head')
- weight_grad: float32 [3072, 3072], P(('tm', 'height'), 'head')
The draws below stay inside these ranges and needn't reach their ends.
Inputs may be any that keep to these rules, and one draw needn't show every extreme that they name: `window`: entry 13, the tile itself, is 1 for every tile. `counts`: every tile outside the last row of height tiles holds 384 valid tokens.
All inputs are finite; a program needn't handle non-finite values.
Results may differ from the reference program's by a relative error of at most 0.023.
Values may be sent and summed in bfloat16 or wider, within the bound.
A program may use at most 128 MiB of HBM per device.

```python
import jax
import jax.numpy as jnp
from jax import lax

D = 3072
HEADS = 24
HDIM = 128
TILE = 384
NW = 1
FT = 4
HT = 2
TILES = 8
TOKENS = 3072


def draw_queries(key, part):
    base_key = jax.random.fold_in(key, 1)
    row_key = jax.random.fold_in(key, 2)
    row_scale = jnp.exp(jax.random.uniform(row_key, (TOKENS, 1), jnp.float32, jnp.log(0.3), jnp.log(1.5)))
    entries = jnp.clip(jax.random.normal(base_key, (TOKENS, HEADS * HDIM), jnp.float32), -4.0, 4.0) * row_scale
    return entries.astype(jnp.bfloat16)


def draw_keys(key, part):
    base_key = jax.random.fold_in(key, 3)
    row_key = jax.random.fold_in(key, 4)
    row_scale = jnp.exp(jax.random.uniform(row_key, (TOKENS, 1), jnp.float32, jnp.log(0.3), jnp.log(3.0)))
    entries = jnp.clip(jax.random.normal(base_key, (TOKENS, HEADS * HDIM), jnp.float32), -4.0, 4.0) * row_scale
    return entries.astype(jnp.bfloat16)


def draw_window(key, part):
    keep_key = jax.random.fold_in(key, 5)
    keep = (jax.random.randint(keep_key, (TILES, 27), 0, 4) < 3).astype(jnp.int32)
    center = (jnp.arange(27, dtype=jnp.int32) == 13)[None, :]
    return jnp.where(center, 1, keep).astype(jnp.int32)


def draw_counts(key, part):
    count_key = jax.random.fold_in(key, 6)
    tile_ids = jnp.arange(TILES, dtype=jnp.int32)
    height_ids = tile_ids // NW % HT
    ragged = jax.random.randint(count_key, (TILES,), TILE // 4, TILE + 1)
    result = jnp.where(height_ids == HT - 1, ragged, TILE)
    result = jnp.where(tile_ids == (HT - 1) * NW, TILE // 4, result)
    return result.astype(jnp.int32)


def strengthened(drawn, stream_key, source, target, parts, factor):
    owner, partner = [(jnp.arange(drawn.shape[dim]) // (drawn.shape[dim] // parts)).reshape([-1 if axis == dim else 1 for axis in range(drawn.ndim)]) for dim in (source, target)]
    chosen = jax.random.permutation(stream_key, parts)[partner]
    strong = (owner == chosen) | (owner == (partner + parts // 2) % parts)
    return jnp.where(strong, factor * drawn, drawn)


def steps_of(key, extent, split, least, largest):
    loudness = 1.0
    for dim, blocks in split:
        steps = jax.random.uniform(jax.random.fold_in(jax.random.fold_in(key, 6), dim), (blocks,), jnp.float32, least / len(split), largest / len(split))
        loudness = loudness * jnp.repeat(jnp.exp(steps), extent[dim] // blocks).reshape((-1,) + (1,) * (len(extent) - 1 - dim))
    return loudness


def scatter_about(rng, dims, deviation, limit, pieces=(), held_as=jnp.bfloat16):
    values = jax.random.normal(rng, dims, jnp.float32) * deviation
    if len(pieces) > 0:
        values = steps_of(rng, dims, pieces, -0.22, 0.18) * values
    return jnp.clip(values, min=-limit, max=limit).astype(held_as)


def gaussian_with(stream_key, extent, deviation, limit, pieces, heavy, kind=jnp.bfloat16):
    values = deviation * jax.random.normal(stream_key, extent, jnp.float32)
    if pieces:
        values = values * steps_of(stream_key, extent, pieces, -0.22, 0.18)
    return jnp.clip(strengthened(values, jax.random.fold_in(stream_key, 3), *heavy), -limit, limit).astype(kind)


def setup_inputs(seed: int = 0) -> dict:
    key_list = jax.random.split(jax.random.key(seed), 8)
    queries = draw_queries(jax.random.fold_in(key_list[7], 71), 0)
    keys = draw_keys(jax.random.fold_in(key_list[7], 71), 0)
    values = scatter_about(key_list[2], (TOKENS, HEADS * HDIM), 1.0, 6.0, ((0, 8), (1, 4)))
    out_grad = gaussian_with(key_list[3], (TOKENS, D), 1.0, 6.0, ((0, 8), (1, 4)), (0, 1, 8, 2.0))
    out_weight = scatter_about(key_list[4], (D, HEADS * HDIM), (HEADS * HDIM) ** -0.5, 0.109375, ((1, 4),))
    window = draw_window(jax.random.fold_in(key_list[7], 71), 0)
    counts = draw_counts(jax.random.fold_in(key_list[7], 71), 0)
    return {"queries": queries, "keys": keys, "values": values, "out_grad": out_grad, "out_weight": out_weight, "window": window, "counts": counts}


neg_large = -1.0e30


def offset_table(width_tiles):
    across = (-1, 0, 1) if width_tiles > 1 else (0,)
    return [(time_step, height_step, width_step) for time_step in (-1, 0, 1) for height_step in (-1, 0, 1) for width_step in across]


def offset_index(offset):
    return (offset[0] + 1) * 9 + (offset[1] + 1) * 3 + offset[2] + 1


def to_heads(source):
    return source.reshape(FT, HT, NW, TILE, HEADS, HDIM).transpose(4, 0, 1, 2, 3, 5)


def from_heads(source):
    return source.transpose(1, 2, 3, 4, 0, 5).reshape(FT * HT * NW * TILE, HEADS * HDIM)


def shifted(padded, offset):
    return padded[1 + offset[0]:1 + offset[0] + FT, 1 + offset[1]:1 + offset[1] + HT, 1 + offset[2]:1 + offset[2] + NW]


def reference(queries, keys, values, out_grad, out_weight, window, counts):
    score_scale = HDIM ** -0.5
    offsets = offset_table(NW)
    grad_out = lax.optimization_barrier(jnp.dot(out_grad, out_weight, preferred_element_type=jnp.float32).astype(jnp.bfloat16))
    positions = jnp.arange(TILE, dtype=jnp.int32)
    key_valid = (positions[None, :] < counts[:, None]).reshape(FT, HT, NW, TILE)
    valid_pad = jnp.pad(key_valid, ((1, 1), (1, 1), (1, 1), (0, 0)))
    window_grid = window.reshape(FT, HT, NW, 27)
    allowed = jnp.concatenate([(window_grid[..., offset_index(offset)] > 0)[..., None] & shifted(valid_pad, offset) for offset in offsets], axis=3)
    pad_grid = ((1, 1), (1, 1), (1, 1), (0, 0), (0, 0))

    def head_pass(operands):
        query_head, key_head, value_head, grad_head = operands
        key_pad = jnp.pad(key_head, pad_grid)
        value_pad = jnp.pad(value_head, pad_grid)
        key_set = jnp.concatenate([shifted(key_pad, offset) for offset in offsets], axis=3).astype(jnp.float32)
        value_set = jnp.concatenate([shifted(value_pad, offset) for offset in offsets], axis=3).astype(jnp.float32)
        query_wide = query_head.astype(jnp.float32)
        grad_wide = grad_head.astype(jnp.float32)
        scores = jnp.einsum("thwid,thwjd->thwij", query_wide, key_set) * score_scale
        scores = jnp.where(allowed[:, :, :, None, :], scores, neg_large)
        row_max = jnp.max(scores, axis=4, keepdims=True)
        row_total = jnp.sum(jnp.exp(scores - row_max), axis=4, keepdims=True)
        log_total = row_max + jnp.log(row_total)
        weights = jnp.exp(scores - log_total)
        weights_low = lax.optimization_barrier(weights.astype(jnp.bfloat16))
        weights_wide = weights_low.astype(jnp.float32)
        attended = lax.optimization_barrier(jnp.einsum("thwij,thwjd->thwid", weights_wide, value_set).astype(jnp.bfloat16))
        row_delta = jnp.sum(grad_wide * attended.astype(jnp.float32), axis=4, keepdims=True)
        grad_weights = jnp.einsum("thwid,thwjd->thwij", grad_wide, value_set)
        grad_scores = lax.optimization_barrier((weights * (grad_weights - row_delta)).astype(jnp.bfloat16))
        scores_wide = grad_scores.astype(jnp.float32)
        query_grad = (jnp.einsum("thwij,thwjd->thwid", scores_wide, key_set) * score_scale).astype(jnp.bfloat16)
        key_part = jnp.einsum("thwij,thwid->thwjd", scores_wide, query_wide)
        value_part = jnp.einsum("thwij,thwid->thwjd", weights_wide, grad_wide)
        key_sum = jnp.zeros(key_pad.shape, jnp.float32)
        value_sum = jnp.zeros(value_pad.shape, jnp.float32)
        for number, offset in enumerate(offsets):
            target = (slice(1 + offset[0], 1 + offset[0] + FT), slice(1 + offset[1], 1 + offset[1] + HT), slice(1 + offset[2], 1 + offset[2] + NW))
            key_sum = key_sum.at[target].add(key_part[:, :, :, number * TILE:(number + 1) * TILE])
            value_sum = value_sum.at[target].add(value_part[:, :, :, number * TILE:(number + 1) * TILE])
        key_grad = (key_sum[1:-1, 1:-1, 1:-1] * score_scale).astype(jnp.bfloat16)
        value_grad = value_sum[1:-1, 1:-1, 1:-1].astype(jnp.bfloat16)
        return query_grad, key_grad, value_grad, attended

    results = lax.map(head_pass, (to_heads(queries), to_heads(keys), to_heads(values), to_heads(grad_out)))
    query_grad = from_heads(results[0])
    key_grad = from_heads(results[1])
    value_grad = from_heads(results[2])
    attended = from_heads(results[3])
    token_total = FT * HT * NW * TILE
    weight_grad = jnp.dot(out_grad.T, attended, preferred_element_type=jnp.float32) * (token_total ** -0.5)
    return (query_grad, key_grad, value_grad, weight_grad)
```

```python
import functools

import jax
import jax.numpy as jnp
from jax import lax
from jax.experimental import pallas as pl
from jax.experimental.pallas import tpu as pltpu
from jax.sharding import PartitionSpec as P

HDIM = 128
TILE = 384
CHUNKS = 2
LOG2E = 1.4426950408889634

neg_large = -1e30


def attention_kernel(slots, bias_ref, query_ref, grad_ref, *refs):
    pair_refs = refs[:slots]
    query_out, attended_out, pair_out, score_ref = refs[slots:]
    scale = HDIM ** (-0.5)
    nt = (((1,), (1,)), ((), ()))
    tn = (((0,), (0,)), ((), ()))
    query = query_ref[...]
    grad = grad_ref[...]
    row_max = None
    for slot in range(slots):
        scores = lax.dot_general(
            query, pair_refs[slot][:TILE], nt, preferred_element_type=jnp.float32
        ) * (scale * LOG2E) + bias_ref[slot]
        score_ref[slot] = scores
        part = jnp.max(scores, axis=1, keepdims=True)
        row_max = part if row_max is None else jnp.maximum(row_max, part)
    total = None
    for slot in range(slots):
        raised = jnp.exp2(score_ref[slot] - row_max)
        score_ref[slot] = raised
        part = jnp.sum(raised, axis=1, keepdims=True)
        total = part if total is None else total + part
    inverse = 1.0 / total
    attended = None
    for slot in range(slots):
        weights = score_ref[slot] * inverse
        score_ref[slot] = weights
        low = weights.astype(jnp.bfloat16)
        part = jnp.dot(low, pair_refs[slot][TILE:], preferred_element_type=jnp.float32)
        attended = part if attended is None else attended + part
        pair_out[slot, TILE:] = lax.dot_general(
            low, grad, tn, preferred_element_type=jnp.float32
        ).astype(jnp.bfloat16)
    attended = attended.astype(jnp.bfloat16)
    attended_out[...] = attended
    delta = jnp.sum(
        grad.astype(jnp.float32) * attended.astype(jnp.float32), axis=1, keepdims=True
    )
    query_sum = None
    for slot in range(slots):
        grad_weights = lax.dot_general(
            grad, pair_refs[slot][TILE:], nt, preferred_element_type=jnp.float32
        )
        grad_scores = (score_ref[slot] * (grad_weights - delta)).astype(jnp.bfloat16)
        part = jnp.dot(grad_scores, pair_refs[slot][:TILE], preferred_element_type=jnp.float32)
        query_sum = part if query_sum is None else query_sum + part
        pair_out[slot, :TILE] = (
            lax.dot_general(grad_scores, query, tn, preferred_element_type=jnp.float32) * scale
        ).astype(jnp.bfloat16)
    query_out[...] = (query_sum * scale).astype(jnp.bfloat16)


def attention(bias, query, grad, pairs):
    slots = len(pairs)
    width = query.shape[1]
    heads = width // HDIM
    rows = pl.BlockSpec((TILE, HDIM), lambda h: (0, h))
    pair = pl.BlockSpec((2 * TILE, HDIM), lambda h: (0, h))
    return pl.pallas_call(
        functools.partial(attention_kernel, slots),
        grid=(heads,),
        in_specs=[pl.BlockSpec((slots, 1, TILE), lambda h: (0, 0, 0)), rows, rows]
        + [pair] * slots,
        out_specs=[rows, rows, pl.BlockSpec((slots, 2 * TILE, HDIM), lambda h: (0, 0, h))],
        out_shape=[
            jax.ShapeDtypeStruct((TILE, width), jnp.bfloat16),
            jax.ShapeDtypeStruct((TILE, width), jnp.bfloat16),
            jax.ShapeDtypeStruct((slots, 2 * TILE, width), jnp.bfloat16),
        ],
        scratch_shapes=[pltpu.VMEM((slots, TILE, TILE), jnp.float32)],
        compiler_params=pltpu.CompilerParams(vmem_limit_bytes=40 * 2**20),
        cost_estimate=pl.CostEstimate(
            flops=heads * slots * 20 * TILE * TILE * HDIM,
            bytes_accessed=heads * slots * 8 * TILE * HDIM,
            transcendentals=heads * slots * TILE * TILE,
        ),
    )(bias, query, grad, *pairs)


def moved(x, axis, by):
    size = lax.axis_size(axis)
    pairs = [(i, i + by) for i in range(size) if 0 <= i + by < size]
    return lax.ppermute(x, axis, pairs)


def swapped(x, axis, bit):
    size = lax.axis_size(axis)
    return lax.ppermute(x, axis, [(i, i ^ (1 << bit)) for i in range(size)])


def height_sends():
    if lax.axis_size("height") == 2:
        swap = functools.partial(swapped, axis="height", bit=0)
        return [(swap, swap)]
    down = functools.partial(moved, axis="height", by=1)
    up = functools.partial(moved, axis="height", by=-1)
    return [(down, up), (up, down)]


def height_steps():
    place = lax.axis_index("height")
    if lax.axis_size("height") == 2:
        return [jnp.int32(0), 1 - 2 * place]
    return [jnp.int32(0), jnp.int32(-1), jnp.int32(1)]


def reduce_scattered(gathered, attended):
    time_size, height_size = lax.axis_size("tm"), lax.axis_size("height")
    time_place, height_place = lax.axis_index("tm"), lax.axis_index("height")
    rows, features = gathered.shape
    block = features // (time_size * height_size)

    def product(part):
        return lax.dot_general(
            part.reshape(rows, -1), attended, (((0,), (0,)), ((), ())),
            preferred_element_type=jnp.float32,
        )

    if time_size & (time_size - 1) or height_size & (height_size - 1) or time_size < 2:
        return lax.psum_scatter(
            product(gathered).astype(jnp.bfloat16), ("tm", "height"),
            scatter_dimension=0, tiled=True,
        ).astype(jnp.float32)
    width = attended.shape[1]
    split = gathered.reshape(rows, time_size // 2, 2, height_size, block)
    bit = time_place % 2

    def half(which):
        part = lax.dynamic_index_in_dim(split, which, 2, keepdims=False)
        return product(part)

    sent = swapped(half(1 - bit).astype(jnp.bfloat16), "tm", 0)
    held = (half(bit) + sent.astype(jnp.float32)).reshape(
        time_size // 2, height_size, block, width
    )
    stages = [("height", number) for number in range(height_size.bit_length() - 1)]
    stages += [("tm", number) for number in range(1, time_size.bit_length() - 1)]
    for axis, number in stages:
        place = height_place if axis == "height" else time_place
        dim = 1 if axis == "height" else 0
        bit = (place // (1 << number)) % 2
        shape = held.shape
        wide = held.reshape(shape[:dim] + (shape[dim] // 2, 2) + shape[dim + 1 :])
        sent = lax.dynamic_index_in_dim(wide, 1 - bit, dim + 1, keepdims=False)
        kept = lax.dynamic_index_in_dim(wide, bit, dim + 1, keepdims=False)
        got = swapped(sent.astype(jnp.bfloat16), axis, number)
        held = kept + got.astype(jnp.float32)
    return held.reshape(block, width)


def on_device(queries, keys, values, out_grad, out_weight, window, counts):
    row_count, width_local = queries.shape
    heads_local = width_local // HDIM
    chunks = CHUNKS if heads_local % CHUNKS == 0 else 1
    width = width_local // chunks
    time_size, height_size = lax.axis_size("tm"), lax.axis_size("height")
    time_place, height_place = lax.axis_index("tm"), lax.axis_index("height")
    sends = height_sends()
    steps = height_steps()
    full_grad = lax.all_gather(out_grad, "head", axis=1, tiled=True)

    def columns(x, chunk):
        return x[:, chunk * width : (chunk + 1) * width]

    packs = []
    for chunk in range(chunks):
        pair = jnp.concatenate([columns(keys, chunk), columns(values, chunk)], axis=0)
        near = [pair] + [fetch(pair) for fetch, _ in sends]
        packs.append(
            near + [moved(x, "tm", 1) for x in near] + [moved(x, "tm", -1) for x in near]
        )
    count_near = [counts] + [fetch(counts) for fetch, _ in sends]
    count_all = (
        count_near
        + [moved(x, "tm", 1) for x in count_near]
        + [moved(x, "tm", -1) for x in count_near]
    )
    positions = jnp.arange(TILE, dtype=jnp.int32)
    rows = []
    number = 0
    for time_step in (0, -1, 1):
        for height_step in steps:
            index = (time_step + 1) * 9 + (height_step + 1) * 3 + 1
            time_at, height_at = time_place + time_step, height_place + height_step
            open_tile = (
                (lax.dynamic_index_in_dim(window[0], index, 0, keepdims=False) > 0)
                & (time_at >= 0)
                & (time_at < time_size)
                & (height_at >= 0)
                & (height_at < height_size)
            )
            rows.append(
                jnp.where(open_tile & (positions < count_all[number]), 0.0, neg_large)[None]
            )
            number += 1
    bias = jnp.stack(rows, axis=0).astype(jnp.float32)
    grad_out = jnp.dot(full_grad, out_weight, preferred_element_type=jnp.float32).astype(
        jnp.bfloat16
    )
    token_share = (row_count * time_size * height_size) ** (-0.5)
    outs = []
    per = len(steps)
    for chunk in range(chunks):
        query_out, attended, pair_out = attention(
            bias, columns(queries, chunk), columns(grad_out, chunk), packs[chunk]
        )
        back = moved(pair_out[per : 2 * per], "tm", -1).astype(jnp.float32)
        ahead = moved(pair_out[2 * per :], "tm", 1).astype(jnp.float32)
        own = pair_out[:per].astype(jnp.float32) + back + ahead
        final = own[0]
        for place, (_, give) in enumerate(sends):
            final = final + give(own[1 + place].astype(jnp.bfloat16)).astype(jnp.float32)
        final = final.astype(jnp.bfloat16)
        weight_out = reduce_scattered(full_grad, attended) * token_share
        outs.append((query_out, final[:TILE], final[TILE:], weight_out))
    return tuple(jnp.concatenate([out[i] for out in outs], axis=1) for i in range(4))


def solution(mesh):
    whole = P(("tm", "height"), "head")
    return jax.shard_map(
        on_device,
        mesh=mesh,
        in_specs=(
            whole,
            whole,
            whole,
            whole,
            P(None, "head"),
            P(("tm", "height"), None),
            P(("tm", "height")),
        ),
        out_specs=(whole,) * 4,
        check_vma=False,
    )
```

```python
import functools

import jax
import jax.numpy as jnp
from jax import lax
from jax.experimental import pallas as pl
from jax.experimental.pallas import tpu as pltpu
from jax.sharding import PartitionSpec as P

HDIM = 128
TILE = 384
CHUNKS = 2
LOG2E = 1.4426950408889634

neg_large = -1e30


nt = (((1,), (1,)), ((), ()))
tn = (((0,), (0,)), ((), ()))
scale = HDIM ** (-0.5)


def forward_kernel(slots, bias_ref, query_ref, *refs):
    pair_refs = refs[:slots]
    attended_out, total_out, score_ref = refs[slots:]
    query = query_ref[...]
    row_max = None
    for slot in range(slots):
        scores = lax.dot_general(
            query, pair_refs[slot][:TILE], nt, preferred_element_type=jnp.float32
        ) * (scale * LOG2E) + bias_ref[slot]
        score_ref[slot] = scores
        part = jnp.max(scores, axis=1, keepdims=True)
        row_max = part if row_max is None else jnp.maximum(row_max, part)
    total = None
    for slot in range(slots):
        raised = jnp.exp2(score_ref[slot] - row_max)
        score_ref[slot] = raised
        part = jnp.sum(raised, axis=1, keepdims=True)
        total = part if total is None else total + part
    total_out[...] = jnp.broadcast_to(row_max + jnp.log2(total), (TILE, HDIM))
    inverse = 1.0 / total
    attended = None
    for slot in range(slots):
        low = (score_ref[slot] * inverse).astype(jnp.bfloat16)
        part = jnp.dot(low, pair_refs[slot][TILE:], preferred_element_type=jnp.float32)
        attended = part if attended is None else attended + part
    attended_out[...] = attended.astype(jnp.bfloat16)


def backward_kernel(slots, bias_ref, query_ref, grad_ref, attended_ref, total_ref, *refs):
    pair_refs = refs[:slots]
    query_out, pair_out = refs[slots:]
    query = query_ref[...]
    grad = grad_ref[...]
    log_total = total_ref[:, :1]
    delta = jnp.sum(
        grad.astype(jnp.float32) * attended_ref[...].astype(jnp.float32), axis=1, keepdims=True
    )
    query_sum = None
    for slot in range(slots):
        key, value = pair_refs[slot][:TILE], pair_refs[slot][TILE:]
        scores = lax.dot_general(query, key, nt, preferred_element_type=jnp.float32) * (
            scale * LOG2E
        ) + bias_ref[slot]
        weights = jnp.exp2(scores - log_total)
        pair_out[slot, TILE:] = lax.dot_general(
            weights.astype(jnp.bfloat16), grad, tn, preferred_element_type=jnp.float32
        ).astype(jnp.bfloat16)
        grad_weights = lax.dot_general(grad, value, nt, preferred_element_type=jnp.float32)
        grad_scores = (weights * (grad_weights - delta)).astype(jnp.bfloat16)
        part = jnp.dot(grad_scores, key, preferred_element_type=jnp.float32)
        query_sum = part if query_sum is None else query_sum + part
        pair_out[slot, :TILE] = (
            lax.dot_general(grad_scores, query, tn, preferred_element_type=jnp.float32) * scale
        ).astype(jnp.bfloat16)
    query_out[...] = (query_sum * scale).astype(jnp.bfloat16)


def specs_of(slots):
    rows = pl.BlockSpec((TILE, HDIM), lambda h: (0, h))
    pair = pl.BlockSpec((2 * TILE, HDIM), lambda h: (0, h))
    return pl.BlockSpec((slots, 1, TILE), lambda h: (0, 0, 0)), rows, [pair] * slots


def forward(bias, query, pairs):
    slots, width = len(pairs), query.shape[1]
    heads = width // HDIM
    bias_spec, rows, pair_specs = specs_of(slots)
    return pl.pallas_call(
        functools.partial(forward_kernel, slots),
        grid=(heads,),
        in_specs=[bias_spec, rows] + pair_specs,
        out_specs=[rows, rows],
        out_shape=[
            jax.ShapeDtypeStruct((TILE, width), jnp.bfloat16),
            jax.ShapeDtypeStruct((TILE, width), jnp.float32),
        ],
        scratch_shapes=[pltpu.VMEM((slots, TILE, TILE), jnp.float32)],
        compiler_params=pltpu.CompilerParams(vmem_limit_bytes=32 * 2**20),
        cost_estimate=pl.CostEstimate(
            flops=heads * slots * 32 * TILE * TILE * HDIM,
            bytes_accessed=heads * slots * 8 * TILE * HDIM,
            transcendentals=heads * slots * TILE * TILE,
        ),
    )(bias, query, *pairs)


def backward(bias, query, grad, attended, total, pairs):
    slots, width = len(pairs), query.shape[1]
    heads = width // HDIM
    bias_spec, rows, pair_specs = specs_of(slots)
    return pl.pallas_call(
        functools.partial(backward_kernel, slots),
        grid=(heads,),
        in_specs=[bias_spec, rows, rows, rows, rows] + pair_specs,
        out_specs=[rows, pl.BlockSpec((slots, 2 * TILE, HDIM), lambda h: (0, 0, h))],
        out_shape=[
            jax.ShapeDtypeStruct((TILE, width), jnp.bfloat16),
            jax.ShapeDtypeStruct((slots, 2 * TILE, width), jnp.bfloat16),
        ],
        compiler_params=pltpu.CompilerParams(vmem_limit_bytes=32 * 2**20),
        cost_estimate=pl.CostEstimate(
            flops=heads * slots * 48 * TILE * TILE * HDIM,
            bytes_accessed=heads * slots * 8 * TILE * HDIM,
            transcendentals=heads * slots * TILE * TILE,
        ),
    )(bias, query, grad, attended, total, *pairs)


def moved(x, axis, by):
    size = lax.axis_size(axis)
    pairs = [(i, i + by) for i in range(size) if 0 <= i + by < size]
    return lax.ppermute(x, axis, pairs)


def swapped(x, axis, bit):
    size = lax.axis_size(axis)
    return lax.ppermute(x, axis, [(i, i ^ (1 << bit)) for i in range(size)])


def height_sends():
    if lax.axis_size("height") == 2:
        swap = functools.partial(swapped, axis="height", bit=0)
        return [(swap, swap)]
    down = functools.partial(moved, axis="height", by=1)
    up = functools.partial(moved, axis="height", by=-1)
    return [(down, up), (up, down)]


def height_steps():
    place = lax.axis_index("height")
    if lax.axis_size("height") == 2:
        return [jnp.int32(0), 1 - 2 * place]
    return [jnp.int32(0), jnp.int32(-1), jnp.int32(1)]


def reduce_scattered(gathered, attended):
    time_size, height_size = lax.axis_size("tm"), lax.axis_size("height")
    time_place, height_place = lax.axis_index("tm"), lax.axis_index("height")
    rows, features = gathered.shape
    block = features // (time_size * height_size)

    def product(part):
        return lax.dot_general(
            part.reshape(rows, -1), attended, (((0,), (0,)), ((), ())),
            preferred_element_type=jnp.float32,
        )

    if time_size & (time_size - 1) or height_size & (height_size - 1) or time_size < 2:
        return [], lax.psum_scatter(
            product(gathered).astype(jnp.bfloat16), ("tm", "height"),
            scatter_dimension=0, tiled=True,
        ).astype(jnp.float32)
    bit = time_place % 2

    def product_of(high, which):
        start = (2 * high + which) * height_size * block
        return product(lax.dynamic_slice_in_dim(gathered, start, height_size * block, 1))

    highs = range(time_size // 2)
    first = [product_of(high, 1 - bit).astype(jnp.bfloat16) for high in highs]
    kept = [product_of(high, bit) for high in highs]
    got = [swapped(x, "tm", 0) for x in first]
    held = [k + g.astype(jnp.float32) for k, g in zip(kept, got)]
    for number in range(height_size.bit_length() - 1):
        bit = (height_place // (1 << number)) % 2
        count = held[0].shape[0] // (2 * block)
        wide = [x.reshape(count, 2, block, -1) for x in held]
        sent = [lax.dynamic_index_in_dim(x, 1 - bit, 1, keepdims=False) for x in wide]
        kept = [lax.dynamic_index_in_dim(x, bit, 1, keepdims=False) for x in wide]
        got = [swapped(x.astype(jnp.bfloat16), "height", number) for x in sent]
        held = [(k + g.astype(jnp.float32)).reshape(count * block, -1) for k, g in zip(kept, got)]
    for number in range(1, time_size.bit_length() - 1):
        bit = (time_place // (1 << number)) % 2
        low, high = held[0::2], held[1::2]
        sent = [jnp.where(bit == 0, y, x) for x, y in zip(low, high)]
        kept = [jnp.where(bit == 0, x, y) for x, y in zip(low, high)]
        got = [swapped(x.astype(jnp.bfloat16), "tm", number) for x in sent]
        held = [k + g.astype(jnp.float32) for k, g in zip(kept, got)]
    return first, held[0]


def on_device(queries, keys, values, out_grad, out_weight, window, counts):
    row_count, width_local = queries.shape
    heads_local = width_local // HDIM
    chunks = CHUNKS if heads_local % CHUNKS == 0 else 1
    width = width_local // chunks
    time_size, height_size = lax.axis_size("tm"), lax.axis_size("height")
    time_place, height_place = lax.axis_index("tm"), lax.axis_index("height")
    sends = height_sends()
    steps = height_steps()
    full_grad = lax.all_gather(out_grad, "head", axis=1, tiled=True)

    def columns(x, chunk):
        return x[:, chunk * width : (chunk + 1) * width]

    packs = []
    for chunk in range(chunks):
        pair = jnp.concatenate([columns(keys, chunk), columns(values, chunk)], axis=0)
        near = [pair] + [fetch(pair) for fetch, _ in sends]
        packs.append(
            near + [moved(x, "tm", 1) for x in near] + [moved(x, "tm", -1) for x in near]
        )
    count_near = [counts] + [fetch(counts) for fetch, _ in sends]
    count_all = (
        count_near
        + [moved(x, "tm", 1) for x in count_near]
        + [moved(x, "tm", -1) for x in count_near]
    )
    positions = jnp.arange(TILE, dtype=jnp.int32)
    rows = []
    number = 0
    for time_step in (0, -1, 1):
        for height_step in steps:
            index = (time_step + 1) * 9 + (height_step + 1) * 3 + 1
            time_at, height_at = time_place + time_step, height_place + height_step
            open_tile = (
                (lax.dynamic_index_in_dim(window[0], index, 0, keepdims=False) > 0)
                & (time_at >= 0)
                & (time_at < time_size)
                & (height_at >= 0)
                & (height_at < height_size)
            )
            rows.append(
                jnp.where(open_tile & (positions < count_all[number]), 0.0, neg_large)[None]
            )
            number += 1
    bias = jnp.stack(rows, axis=0).astype(jnp.float32)
    grad_out = jnp.dot(full_grad, out_weight, preferred_element_type=jnp.float32).astype(
        jnp.bfloat16
    )
    token_share = (row_count * time_size * height_size) ** (-0.5)
    per = len(steps)
    ahead_of = [forward(bias, columns(queries, c), packs[c]) for c in range(chunks)]
    attended_all = jnp.concatenate([x[0] for x in ahead_of], axis=1)
    first, weight_out = reduce_scattered(full_grad, attended_all)
    grad_out, first = lax.optimization_barrier((grad_out, first))
    outs = []
    for chunk in range(chunks):
        attended, total = ahead_of[chunk]
        query_out, pair_out = backward(
            bias, columns(queries, chunk), columns(grad_out, chunk), attended, total, packs[chunk]
        )
        back = moved(pair_out[per : 2 * per], "tm", -1).astype(jnp.float32)
        ahead = moved(pair_out[2 * per :], "tm", 1).astype(jnp.float32)
        own = pair_out[:per].astype(jnp.float32) + back + ahead
        final = own[0]
        for place, (_, give) in enumerate(sends):
            final = final + give(own[1 + place].astype(jnp.bfloat16)).astype(jnp.float32)
        final = final.astype(jnp.bfloat16)
        outs.append((query_out, final[:TILE], final[TILE:]))
    joined = tuple(jnp.concatenate([out[i] for out in outs], axis=1) for i in range(3))
    return joined + (weight_out * token_share,)


def solution(mesh):
    whole = P(("tm", "height"), "head")
    return jax.shard_map(
        on_device,
        mesh=mesh,
        in_specs=(
            whole,
            whole,
            whole,
            whole,
            P(None, "head"),
            P(("tm", "height"), None),
            P(("tm", "height")),
        ),
        out_specs=(whole,) * 4,
        check_vma=False,
    )
```

```python
import functools

import jax
import jax.numpy as jnp
from jax import lax
from jax.experimental import pallas as pl
from jax.experimental.pallas import tpu as pltpu
from jax.sharding import PartitionSpec as P

HDIM = 128
TILE = 384
CHUNKS = 2
LOG2E = 1.4426950408889634

neg_large = -1e30


nt = (((1,), (1,)), ((), ()))
tn = (((0,), (0,)), ((), ()))
scale = HDIM ** (-0.5)


def forward_kernel(slots, bias_ref, query_ref, *refs):
    pair_refs = refs[:slots]
    attended_out, total_out, score_ref = refs[slots:]
    query = query_ref[...]
    row_max = None
    for slot in range(slots):
        scores = lax.dot_general(
            query, pair_refs[slot][:TILE], nt, preferred_element_type=jnp.float32
        ) * (scale * LOG2E) + bias_ref[slot]
        score_ref[slot] = scores
        part = jnp.max(scores, axis=1, keepdims=True)
        row_max = part if row_max is None else jnp.maximum(row_max, part)
    total = None
    for slot in range(slots):
        raised = jnp.exp2(score_ref[slot] - row_max)
        score_ref[slot] = raised
        part = jnp.sum(raised, axis=1, keepdims=True)
        total = part if total is None else total + part
    total_out[...] = jnp.broadcast_to(row_max + jnp.log2(total), (TILE, HDIM))
    inverse = 1.0 / total
    attended = None
    for slot in range(slots):
        low = (score_ref[slot] * inverse).astype(jnp.bfloat16)
        part = jnp.dot(low, pair_refs[slot][TILE:], preferred_element_type=jnp.float32)
        attended = part if attended is None else attended + part
    attended_out[...] = attended.astype(jnp.bfloat16)


def backward_kernel(slots, bias_ref, query_ref, grad_ref, attended_ref, total_ref, *refs):
    pair_refs = refs[:slots]
    query_out, pair_out = refs[slots:]
    query = query_ref[...]
    grad = grad_ref[...]
    log_total = total_ref[:, :1]
    delta = jnp.sum(
        grad.astype(jnp.float32) * attended_ref[...].astype(jnp.float32), axis=1, keepdims=True
    )
    query_sum = None
    for slot in range(slots):
        key, value = pair_refs[slot][:TILE], pair_refs[slot][TILE:]
        scores = lax.dot_general(query, key, nt, preferred_element_type=jnp.float32) * (
            scale * LOG2E
        ) + bias_ref[slot]
        weights = jnp.exp2(scores - log_total)
        pair_out[slot, TILE:] = lax.dot_general(
            weights.astype(jnp.bfloat16), grad, tn, preferred_element_type=jnp.float32
        ).astype(jnp.bfloat16)
        grad_weights = lax.dot_general(grad, value, nt, preferred_element_type=jnp.float32)
        grad_scores = (weights * (grad_weights - delta)).astype(jnp.bfloat16)
        part = jnp.dot(grad_scores, key, preferred_element_type=jnp.float32)
        query_sum = part if query_sum is None else query_sum + part
        pair_out[slot, :TILE] = (
            lax.dot_general(grad_scores, query, tn, preferred_element_type=jnp.float32) * scale
        ).astype(jnp.bfloat16)
    query_out[...] = (query_sum * scale).astype(jnp.bfloat16)


def specs_of(slots):
    rows = pl.BlockSpec((TILE, HDIM), lambda h: (0, h))
    pair = pl.BlockSpec((2 * TILE, HDIM), lambda h: (0, h))
    return pl.BlockSpec((slots, 1, TILE), lambda h: (0, 0, 0)), rows, [pair] * slots


def forward(bias, query, pairs):
    slots, width = len(pairs), query.shape[1]
    heads = width // HDIM
    bias_spec, rows, pair_specs = specs_of(slots)
    return pl.pallas_call(
        functools.partial(forward_kernel, slots),
        grid=(heads,),
        in_specs=[bias_spec, rows] + pair_specs,
        out_specs=[rows, rows],
        out_shape=[
            jax.ShapeDtypeStruct((TILE, width), jnp.bfloat16),
            jax.ShapeDtypeStruct((TILE, width), jnp.float32),
        ],
        scratch_shapes=[pltpu.VMEM((slots, TILE, TILE), jnp.float32)],
        compiler_params=pltpu.CompilerParams(vmem_limit_bytes=32 * 2**20),
        cost_estimate=pl.CostEstimate(
            flops=heads * slots * 32 * TILE * TILE * HDIM,
            bytes_accessed=heads * slots * 8 * TILE * HDIM,
            transcendentals=heads * slots * TILE * TILE,
        ),
    )(bias, query, *pairs)


def backward(bias, query, grad, attended, total, pairs):
    slots, width = len(pairs), query.shape[1]
    heads = width // HDIM
    bias_spec, rows, pair_specs = specs_of(slots)
    return pl.pallas_call(
        functools.partial(backward_kernel, slots),
        grid=(heads,),
        in_specs=[bias_spec, rows, rows, rows, rows] + pair_specs,
        out_specs=[rows, pl.BlockSpec((slots, 2 * TILE, HDIM), lambda h: (0, 0, h))],
        out_shape=[
            jax.ShapeDtypeStruct((TILE, width), jnp.bfloat16),
            jax.ShapeDtypeStruct((slots, 2 * TILE, width), jnp.bfloat16),
        ],
        compiler_params=pltpu.CompilerParams(vmem_limit_bytes=32 * 2**20),
        cost_estimate=pl.CostEstimate(
            flops=heads * slots * 48 * TILE * TILE * HDIM,
            bytes_accessed=heads * slots * 8 * TILE * HDIM,
            transcendentals=heads * slots * TILE * TILE,
        ),
    )(bias, query, grad, attended, total, *pairs)


def moved(x, axis, by):
    size = lax.axis_size(axis)
    pairs = [(i, i + by) for i in range(size) if 0 <= i + by < size]
    return lax.ppermute(x, axis, pairs)


def swapped(x, axis, bit):
    size = lax.axis_size(axis)
    return lax.ppermute(x, axis, [(i, i ^ (1 << bit)) for i in range(size)])


def height_sends():
    if lax.axis_size("height") == 2:
        swap = functools.partial(swapped, axis="height", bit=0)
        return [(swap, swap)]
    down = functools.partial(moved, axis="height", by=1)
    up = functools.partial(moved, axis="height", by=-1)
    return [(down, up), (up, down)]


def height_steps():
    place = lax.axis_index("height")
    if lax.axis_size("height") == 2:
        return [jnp.int32(0), 1 - 2 * place]
    return [jnp.int32(0), jnp.int32(-1), jnp.int32(1)]


def reduce_scattered(gathered, attended):
    time_size, height_size = lax.axis_size("tm"), lax.axis_size("height")
    time_place, height_place = lax.axis_index("tm"), lax.axis_index("height")
    rows, features = gathered.shape
    block = features // (time_size * height_size)

    def product(part):
        return lax.dot_general(
            part.reshape(rows, -1), attended, (((0,), (0,)), ((), ())),
            preferred_element_type=jnp.float32,
        )

    if time_size & (time_size - 1) or height_size & (height_size - 1) or time_size < 2:
        return [], [], lax.psum_scatter(
            product(gathered).astype(jnp.bfloat16), ("tm", "height"),
            scatter_dimension=0, tiled=True,
        ).astype(jnp.float32)
    bit = time_place % 2
    span = height_size * block

    def product_of(which):
        parts = [
            lax.dynamic_slice_in_dim(gathered, (2 * high + which) * span, span, 1)
            for high in range(time_size // 2)
        ]
        return product(jnp.concatenate(parts, axis=1))

    got = swapped(product_of(1 - bit).astype(jnp.bfloat16), "tm", 0)
    held = product_of(bit) + got.astype(jnp.float32)

    def rows_for(time_mask, height_mask):
        owner = (time_place // 2 ^ time_mask) * height_size + (height_place ^ height_mask)
        return lax.dynamic_slice_in_dim(held, owner * block, block, 0)

    masks = [(t, h) for t in range(time_size // 2) for h in range(height_size)][1:]
    sent = [rows_for(*mask).astype(jnp.bfloat16) for mask in masks]
    return masks, sent, rows_for(0, 0)


def exchanged(masks, sent):
    time_size, height_size = lax.axis_size("tm"), lax.axis_size("height")
    got = []
    for (time_mask, height_mask), x in zip(masks, sent):
        pairs = [
            (t * height_size + h, (t ^ (2 * time_mask)) * height_size + (h ^ height_mask))
            for t in range(time_size)
            for h in range(height_size)
        ]
        got.append(lax.ppermute(x, ("tm", "height"), pairs))
    return got


def on_device(queries, keys, values, out_grad, out_weight, window, counts):
    row_count, width_local = queries.shape
    heads_local = width_local // HDIM
    chunks = CHUNKS if heads_local % CHUNKS == 0 and heads_local > CHUNKS else 1
    width = width_local // chunks
    time_size, height_size = lax.axis_size("tm"), lax.axis_size("height")
    time_place, height_place = lax.axis_index("tm"), lax.axis_index("height")
    sends = height_sends()
    steps = height_steps()
    full_grad = lax.all_gather(out_grad, "head", axis=1, tiled=True)

    def columns(x, chunk):
        return x[:, chunk * width : (chunk + 1) * width]

    packs = []
    for chunk in range(chunks):
        parts = [columns(keys, chunk), columns(values, chunk)]
        if chunk == 0:
            parts.append(
                jnp.where(jnp.arange(width) < HDIM, counts // 16, counts % 16)[None]
                .astype(jnp.bfloat16)
                .repeat(16, axis=0)
            )
        pair = jnp.concatenate(parts, axis=0)
        near = [pair] + [fetch(pair) for fetch, _ in sends]
        packs.append(
            near + [moved(x, "tm", 1) for x in near] + [moved(x, "tm", -1) for x in near]
        )
    count_all = [
        (x[2 * TILE, 0].astype(jnp.int32) * 16 + x[2 * TILE, width - 1].astype(jnp.int32))
        for x in packs[0]
    ]
    positions = jnp.arange(TILE, dtype=jnp.int32)
    rows = []
    number = 0
    for time_step in (0, -1, 1):
        for height_step in steps:
            index = (time_step + 1) * 9 + (height_step + 1) * 3 + 1
            time_at, height_at = time_place + time_step, height_place + height_step
            open_tile = (
                (lax.dynamic_index_in_dim(window[0], index, 0, keepdims=False) > 0)
                & (time_at >= 0)
                & (time_at < time_size)
                & (height_at >= 0)
                & (height_at < height_size)
            )
            rows.append(
                jnp.where(open_tile & (positions < count_all[number]), 0.0, neg_large)[None]
            )
            number += 1
    bias = jnp.stack(rows, axis=0).astype(jnp.float32)
    grad_out = jnp.dot(full_grad, out_weight, preferred_element_type=jnp.float32).astype(
        jnp.bfloat16
    )
    token_share = (row_count * time_size * height_size) ** (-0.5)
    per = len(steps)
    ahead_of = [forward(bias, columns(queries, c), packs[c]) for c in range(chunks)]
    attended_all = jnp.concatenate([x[0] for x in ahead_of], axis=1)
    masks, sent, kept = reduce_scattered(full_grad, attended_all)
    grad_out, sent = lax.optimization_barrier((grad_out, sent))
    got = exchanged(masks, sent)
    outs = []
    for chunk in range(chunks):
        attended, total = ahead_of[chunk]
        grad_part = columns(grad_out, chunk)
        if chunk > 0:
            grad_part, got[:2] = lax.optimization_barrier((grad_part, got[:2]))
        query_out, pair_out = backward(
            bias, columns(queries, chunk), grad_part, attended, total, packs[chunk]
        )
        back = moved(pair_out[per : 2 * per], "tm", -1).astype(jnp.float32)
        ahead = moved(pair_out[2 * per :], "tm", 1).astype(jnp.float32)
        own = pair_out[:per].astype(jnp.float32) + back + ahead
        final = own[0]
        for place, (_, give) in enumerate(sends):
            final = final + give(own[1 + place].astype(jnp.bfloat16)).astype(jnp.float32)
        final = final.astype(jnp.bfloat16)
        outs.append((query_out, final[:TILE], final[TILE:]))
    joined = tuple(jnp.concatenate([out[i] for out in outs], axis=1) for i in range(3))
    weight_out = kept + sum(x.astype(jnp.float32) for x in got)
    return joined + (weight_out * token_share,)


def solution(mesh):
    whole = P(("tm", "height"), "head")
    return jax.shard_map(
        on_device,
        mesh=mesh,
        in_specs=(
            whole,
            whole,
            whole,
            whole,
            P(None, "head"),
            P(("tm", "height"), None),
            P(("tm", "height")),
        ),
        out_specs=(whole,) * 4,
        check_vma=False,
    )
```

```python
import functools

import jax
import jax.numpy as jnp
from jax import lax
from jax.experimental import pallas as pl
from jax.experimental.pallas import tpu as pltpu
from jax.sharding import PartitionSpec as P

HDIM = 128
TILE = 384
LOG2E = 1.4426950408889634

neg_large = -1e30


nt = (((1,), (1,)), ((), ()))
tn = (((0,), (0,)), ((), ()))
scale = HDIM ** (-0.5)


def forward_kernel(slots, bias_ref, query_ref, *refs):
    pair_refs = refs[:slots]
    attended_out, total_out, score_ref = refs[slots:]
    query = query_ref[...]
    row_max = None
    for slot in range(slots):
        scores = lax.dot_general(
            query, pair_refs[slot][:TILE], nt, preferred_element_type=jnp.float32
        ) * (scale * LOG2E) + bias_ref[slot]
        score_ref[slot] = scores
        part = jnp.max(scores, axis=1, keepdims=True)
        row_max = part if row_max is None else jnp.maximum(row_max, part)
    total = None
    for slot in range(slots):
        raised = jnp.exp2(score_ref[slot] - row_max)
        score_ref[slot] = raised
        part = jnp.sum(raised, axis=1, keepdims=True)
        total = part if total is None else total + part
    total_out[...] = jnp.broadcast_to(row_max + jnp.log2(total), (TILE, HDIM))
    inverse = 1.0 / total
    attended = None
    for slot in range(slots):
        low = (score_ref[slot] * inverse).astype(jnp.bfloat16)
        part = jnp.dot(low, pair_refs[slot][TILE:], preferred_element_type=jnp.float32)
        attended = part if attended is None else attended + part
    attended_out[...] = attended.astype(jnp.bfloat16)


def backward_kernel(slots, bias_ref, query_ref, grad_ref, attended_ref, total_ref, *refs):
    pair_refs = refs[:slots]
    query_out, pair_out = refs[slots:]
    query = query_ref[...]
    grad = grad_ref[...]
    log_total = total_ref[:, :1]
    delta = jnp.sum(
        grad.astype(jnp.float32) * attended_ref[...].astype(jnp.float32), axis=1, keepdims=True
    )
    query_sum = None
    for slot in range(slots):
        key, value = pair_refs[slot][:TILE], pair_refs[slot][TILE:]
        scores = lax.dot_general(query, key, nt, preferred_element_type=jnp.float32) * (
            scale * LOG2E
        ) + bias_ref[slot]
        weights = jnp.exp2(scores - log_total)
        pair_out[slot, TILE:] = lax.dot_general(
            weights.astype(jnp.bfloat16), grad, tn, preferred_element_type=jnp.float32
        ).astype(jnp.bfloat16)
        grad_weights = lax.dot_general(grad, value, nt, preferred_element_type=jnp.float32)
        grad_scores = (weights * (grad_weights - delta)).astype(jnp.bfloat16)
        part = jnp.dot(grad_scores, key, preferred_element_type=jnp.float32)
        query_sum = part if query_sum is None else query_sum + part
        pair_out[slot, :TILE] = (
            lax.dot_general(grad_scores, query, tn, preferred_element_type=jnp.float32) * scale
        ).astype(jnp.bfloat16)
    query_out[...] = (query_sum * scale).astype(jnp.bfloat16)


def specs_of(slots):
    rows = pl.BlockSpec((TILE, HDIM), lambda h: (0, h))
    pair = pl.BlockSpec((2 * TILE, HDIM), lambda h: (0, h))
    return pl.BlockSpec((slots, 1, TILE), lambda h: (0, 0, 0)), rows, [pair] * slots


def forward(bias, query, pairs):
    slots, width = len(pairs), query.shape[1]
    heads = width // HDIM
    bias_spec, rows, pair_specs = specs_of(slots)
    return pl.pallas_call(
        functools.partial(forward_kernel, slots),
        grid=(heads,),
        in_specs=[bias_spec, rows] + pair_specs,
        out_specs=[rows, rows],
        out_shape=[
            jax.ShapeDtypeStruct((TILE, width), jnp.bfloat16),
            jax.ShapeDtypeStruct((TILE, width), jnp.float32),
        ],
        scratch_shapes=[pltpu.VMEM((slots, TILE, TILE), jnp.float32)],
        compiler_params=pltpu.CompilerParams(vmem_limit_bytes=32 * 2**20),
        cost_estimate=pl.CostEstimate(
            flops=heads * slots * 32 * TILE * TILE * HDIM,
            bytes_accessed=heads * slots * 8 * TILE * HDIM,
            transcendentals=heads * slots * TILE * TILE,
        ),
    )(bias, query, *pairs)


def backward(bias, query, grad, attended, total, pairs):
    slots, width = len(pairs), query.shape[1]
    heads = width // HDIM
    bias_spec, rows, pair_specs = specs_of(slots)
    return pl.pallas_call(
        functools.partial(backward_kernel, slots),
        grid=(heads,),
        in_specs=[bias_spec, rows, rows, rows, rows] + pair_specs,
        out_specs=[rows, pl.BlockSpec((slots, 2 * TILE, HDIM), lambda h: (0, 0, h))],
        out_shape=[
            jax.ShapeDtypeStruct((TILE, width), jnp.bfloat16),
            jax.ShapeDtypeStruct((slots, 2 * TILE, width), jnp.bfloat16),
        ],
        compiler_params=pltpu.CompilerParams(vmem_limit_bytes=32 * 2**20),
        cost_estimate=pl.CostEstimate(
            flops=heads * slots * 48 * TILE * TILE * HDIM,
            bytes_accessed=heads * slots * 8 * TILE * HDIM,
            transcendentals=heads * slots * TILE * TILE,
        ),
    )(bias, query, grad, attended, total, *pairs)


def moved(x, axis, by):
    size = lax.axis_size(axis)
    pairs = [(i, i + by) for i in range(size) if 0 <= i + by < size]
    return lax.ppermute(x, axis, pairs)


def swapped(x, axis, bit):
    size = lax.axis_size(axis)
    return lax.ppermute(x, axis, [(i, i ^ (1 << bit)) for i in range(size)])


def height_sends():
    if lax.axis_size("height") == 2:
        swap = functools.partial(swapped, axis="height", bit=0)
        return [(swap, swap)]
    down = functools.partial(moved, axis="height", by=1)
    up = functools.partial(moved, axis="height", by=-1)
    return [(down, up), (up, down)]


def height_steps():
    place = lax.axis_index("height")
    if lax.axis_size("height") == 2:
        return [jnp.int32(0), 1 - 2 * place]
    return [jnp.int32(0), jnp.int32(-1), jnp.int32(1)]


def reduce_scattered(gathered, attended):
    time_size, height_size = lax.axis_size("tm"), lax.axis_size("height")
    time_place, height_place = lax.axis_index("tm"), lax.axis_index("height")
    rows, features = gathered.shape
    block = features // (time_size * height_size)

    def product(part):
        return lax.dot_general(
            part.reshape(rows, -1), attended, (((0,), (0,)), ((), ())),
            preferred_element_type=jnp.float32,
        )

    if time_size & (time_size - 1) or height_size & (height_size - 1) or time_size < 2:
        return [], [], lax.psum_scatter(
            product(gathered).astype(jnp.bfloat16), ("tm", "height"),
            scatter_dimension=0, tiled=True,
        ).astype(jnp.float32)
    bit = time_place % 2
    span = height_size * block

    def product_of(which):
        parts = [
            lax.dynamic_slice_in_dim(gathered, (2 * high + which) * span, span, 1)
            for high in range(time_size // 2)
        ]
        return product(jnp.concatenate(parts, axis=1))

    got = swapped(product_of(1 - bit).astype(jnp.bfloat16), "tm", 0)
    held = product_of(bit) + got.astype(jnp.float32)

    def rows_for(time_mask, height_mask):
        owner = (time_place // 2 ^ time_mask) * height_size + (height_place ^ height_mask)
        return lax.dynamic_slice_in_dim(held, owner * block, block, 0)

    masks = [(t, h) for t in range(time_size // 2) for h in range(height_size)][1:]
    sent = [rows_for(*mask).astype(jnp.bfloat16) for mask in masks]
    return masks, sent, rows_for(0, 0)


def exchanged(masks, sent):
    time_size, height_size = lax.axis_size("tm"), lax.axis_size("height")
    got = []
    for (time_mask, height_mask), x in zip(masks, sent):
        pairs = [
            (t * height_size + h, (t ^ (2 * time_mask)) * height_size + (h ^ height_mask))
            for t in range(time_size)
            for h in range(height_size)
        ]
        got.append(lax.ppermute(x, ("tm", "height"), pairs))
    return got


def on_device(queries, keys, values, out_grad, out_weight, window, counts):
    row_count, width_local = queries.shape
    heads_local = width_local // HDIM
    first_heads = max(heads_local - heads_local // 3, min(heads_local, 2))
    bounds = [(0, first_heads * HDIM), (first_heads * HDIM, width_local)]
    bounds = [(low, high) for low, high in bounds if high > low]
    chunks = len(bounds)
    time_size, height_size = lax.axis_size("tm"), lax.axis_size("height")
    time_place, height_place = lax.axis_index("tm"), lax.axis_index("height")
    sends = height_sends()
    steps = height_steps()
    full_grad = lax.all_gather(out_grad, "head", axis=1, tiled=True)

    def columns(x, chunk):
        low, high = bounds[chunk]
        return x[:, low:high]

    packs = []
    for chunk in range(chunks):
        parts = [columns(keys, chunk), columns(values, chunk)]
        if chunk == 0:
            parts.append(
                jnp.where(jnp.arange(bounds[0][1]) < HDIM, counts // 16, counts % 16)[None]
                .astype(jnp.bfloat16)
                .repeat(16, axis=0)
            )
        pair = jnp.concatenate(parts, axis=0)
        near = [pair] + [fetch(pair) for fetch, _ in sends]
        packs.append(
            near + [moved(x, "tm", 1) for x in near] + [moved(x, "tm", -1) for x in near]
        )
    count_all = [
        (x[2 * TILE, 0].astype(jnp.int32) * 16 + x[2 * TILE, bounds[0][1] - 1].astype(jnp.int32))
        for x in packs[0]
    ]
    positions = jnp.arange(TILE, dtype=jnp.int32)
    rows = []
    number = 0
    for time_step in (0, -1, 1):
        for height_step in steps:
            index = (time_step + 1) * 9 + (height_step + 1) * 3 + 1
            time_at, height_at = time_place + time_step, height_place + height_step
            open_tile = (
                (lax.dynamic_index_in_dim(window[0], index, 0, keepdims=False) > 0)
                & (time_at >= 0)
                & (time_at < time_size)
                & (height_at >= 0)
                & (height_at < height_size)
            )
            rows.append(
                jnp.where(open_tile & (positions < count_all[number]), 0.0, neg_large)[None]
            )
            number += 1
    bias = jnp.stack(rows, axis=0).astype(jnp.float32)
    grad_out = jnp.dot(full_grad, out_weight, preferred_element_type=jnp.float32).astype(
        jnp.bfloat16
    )
    token_share = (row_count * time_size * height_size) ** (-0.5)
    per = len(steps)
    ahead_of = [forward(bias, columns(queries, c), packs[c]) for c in range(chunks)]
    attended_all = jnp.concatenate([x[0] for x in ahead_of], axis=1)
    masks, sent, kept = reduce_scattered(full_grad, attended_all)
    grad_out, sent = lax.optimization_barrier((grad_out, sent))
    got = exchanged(masks, sent)
    outs = []

    def height_returned(query_out, final, height_sent):
        for (_, give), x in zip(sends, height_sent):
            final = final + give(x).astype(jnp.float32)
        final = final.astype(jnp.bfloat16)
        return query_out, final[:TILE], final[TILE:]

    for chunk in range(chunks):
        attended, total = ahead_of[chunk]
        grad_part = columns(grad_out, chunk)
        if chunk > 0:
            grad_part, got[:2] = lax.optimization_barrier((grad_part, got[:2]))
        query_out, pair_out = backward(
            bias, columns(queries, chunk), grad_part, attended, total, packs[chunk]
        )
        if chunk > 0:
            pair_out, height_sent = lax.optimization_barrier((pair_out, height_sent))
            outs.append(height_returned(kept_query, kept_own, height_sent))
        back = moved(pair_out[per : 2 * per], "tm", -1).astype(jnp.float32)
        ahead = moved(pair_out[2 * per :], "tm", 1).astype(jnp.float32)
        own = pair_out[:per].astype(jnp.float32) + back + ahead
        height_sent = [own[1 + place].astype(jnp.bfloat16) for place in range(per - 1)]
        kept_query, kept_own = query_out, own[0]
    outs.append(height_returned(kept_query, kept_own, height_sent))
    joined = tuple(jnp.concatenate([out[i] for out in outs], axis=1) for i in range(3))
    weight_out = kept + sum(x.astype(jnp.float32) for x in got)
    return joined + (weight_out * token_share,)


def solution(mesh):
    whole = P(("tm", "height"), "head")
    return jax.shard_map(
        on_device,
        mesh=mesh,
        in_specs=(
            whole,
            whole,
            whole,
            whole,
            P(None, "head"),
            P(("tm", "height"), None),
            P(("tm", "height")),
        ),
        out_specs=(whole,) * 4,
        check_vma=False,
    )
```
